32 devices in a mesh: group: 2 (over x), dp: 16 (over z, y, core).
Axes of the slice: x: 2, y: 2, z: 4, core: 2. Of those that a mesh axis runs over, the one named last changes fastest.
Arguments:
- hidden_in: bfloat16 [1024, 5120], P('group', 'dp'), parts along dimension 0, may hold values from -6 to 6
- w_gate: bfloat16 [5120, 13824], P(None, 'dp'), may hold values from -0.078125 to 0.078125
- w_up: bfloat16 [5120, 13824], P(None, 'dp'), may hold values from -0.078125 to 0.078125
- w_down: bfloat16 [13824, 5120], P('dp'), may hold values from -0.0546875 to 0.0546875
- norm_gain: float32 [5120], replicated, may hold values from 0.25 to 1.75
- out_cotangent: bfloat16 [1024, 5120], P('group', 'dp'), parts along dimension 0, may hold values from -6 to 6
- proj_model: bfloat16 [3, 64, 5120], replicated, may hold values from -0.078125 to 0.078125
- proj_hidden: bfloat16 [3, 64, 13824], P(None, None, 'dp'), may hold values from -0.0546875 to 0.0546875
- queries: bfloat16 [1024, 12288], P('dp'), may hold values from -0.0546875 to 0.0546875
Outputs:
- block_out: bfloat16 [1024, 5120], P('group', 'dp'), parts along dimension 0
- scores: float32 [4, 1024], P('group', 'dp'), parts along dimension 0
The draws below stay inside these ranges and needn't reach their ends.
There are 2 independent parts, one for each index of `group`. The reference program is written for one: setup_inputs(seed, part) draws one part's arguments, and reference() takes and returns one part's arrays. A program takes and returns all parts, laid end to end along the dimension named above; an argument that names none is the same for every part. Nothing has to cross between parts.
All inputs are finite; a program needn't handle non-finite values.
Results may differ from the reference program's by a relative error of at most 0.005.
Values may be sent and summed in bfloat16 or wider, within the bound.
A program may use at most 128 MiB of HBM per device.

```python
import jax
import jax.numpy as jnp
from jax import lax

D = 5120
FF = 13824
K = 64
SEQ = 256
NSEQ = 2
TOKENS = 512
QUERIES = 1024
FEATS = 12288


def block_levels(rng, dims, shards, low, high):
    def one(axis_at, shards_of):
        heights = jax.random.uniform(jax.random.fold_in(jax.random.fold_in(rng, 6), axis_at), (shards_of,), jnp.float32, low / len(shards), high / len(shards))
        return jnp.repeat(jnp.exp(heights), dims[axis_at] // shards_of).reshape((-1,) + (1,) * (len(dims) - axis_at - 1))

    gain = one(*shards[0])
    for cut in shards[1:]:
        gain = gain * one(*cut)
    return gain


def bell_draw(key, dims, scale, most, pieces=(), dtype=jnp.bfloat16):
    drawn = jax.random.normal(key, dims, jnp.float32) * scale
    if len(pieces) > 0:
        drawn = block_levels(key, dims, pieces, -0.22, 0.18) * drawn
    return jnp.clip(drawn, min=-most, max=most).astype(dtype)


def setup_inputs(seed: int = 0, part: int = 0) -> dict:
    streams_of = jax.random.split(jax.random.key(seed), 10)
    own_keys = jax.random.split(jax.random.fold_in(streams_of[9], part), 10)
    return {
        "hidden_in": bell_draw(own_keys[0], (TOKENS, D), 1.0, 6.0, ((1, 16),)),
        "w_gate": bell_draw(streams_of[1], (D, FF), D ** -0.5, 0.078125, ((1, 16),)),
        "w_up": bell_draw(streams_of[2], (D, FF), D ** -0.5, 0.078125, ((1, 16),)),
        "w_down": bell_draw(streams_of[3], (FF, D), FF ** -0.5, 0.0546875, ((0, 16),)),
        "norm_gain": jnp.clip(1.0 + 0.15 * jax.random.normal(streams_of[4], (D,), jnp.float32), 0.25, 1.75),
        "out_cotangent": bell_draw(own_keys[5], (TOKENS, D), 1.0, 6.0, ((1, 16),)),
        "proj_model": bell_draw(streams_of[6], (3, K, D), D ** -0.5, 0.078125),
        "proj_hidden": bell_draw(streams_of[7], (3, K, FF), FF ** -0.5, 0.0546875, ((2, 16),)),
        "queries": bell_draw(streams_of[8], (QUERIES, FEATS), FEATS ** -0.5, 0.0546875, ((0, 16),)),
    }


epsilon = 1e-06

def pair_sketch(inputs_side, grads_side):
    inputs_seq = inputs_side.reshape(NSEQ, SEQ, K)
    grads_seq = grads_side.reshape(NSEQ, SEQ, K)
    return jnp.einsum('stk,stj->skj', inputs_seq, grads_seq, precision=lax.Precision.HIGHEST)

def reference(hidden_in, w_gate, w_up, w_down, norm_gain, out_cotangent, proj_model, proj_hidden, queries):
    gate_value = jnp.dot(hidden_in, w_gate, preferred_element_type=jnp.float32)
    up_value = jnp.dot(hidden_in, w_up, preferred_element_type=jnp.float32)
    sigmoid_gate = jax.nn.sigmoid(gate_value)
    activated = gate_value * sigmoid_gate
    hidden = (activated * up_value).astype(jnp.bfloat16)
    down_sum = jnp.dot(hidden, w_down, preferred_element_type=jnp.float32)
    inv_rms = lax.rsqrt(lax.optimization_barrier(jnp.mean(down_sum * down_sum, axis=1, keepdims=True)) + epsilon)
    block_out = (hidden_in.astype(jnp.float32) + down_sum * inv_rms * norm_gain).astype(jnp.bfloat16)
    scaled = norm_gain * out_cotangent.astype(jnp.float32)
    mixed_mean = lax.optimization_barrier(jnp.mean(scaled * down_sum, axis=1, keepdims=True))
    grad_down = (inv_rms * (scaled - down_sum * inv_rms * inv_rms * mixed_mean)).astype(jnp.bfloat16)
    grad_hidden = jnp.dot(grad_down, w_down.T, preferred_element_type=jnp.float32)
    grad_up = (grad_hidden * activated).astype(jnp.bfloat16)
    grad_gate = (grad_hidden * up_value * sigmoid_gate * (1.0 + gate_value * (1.0 - sigmoid_gate))).astype(jnp.bfloat16)
    in_gate = jnp.dot(hidden_in, proj_model[0].T, preferred_element_type=jnp.float32)
    in_up = jnp.dot(hidden_in, proj_model[1].T, preferred_element_type=jnp.float32)
    out_down = jnp.dot(grad_down, proj_model[2].T, preferred_element_type=jnp.float32)
    out_gate = jnp.dot(grad_gate, proj_hidden[0].T, preferred_element_type=jnp.float32)
    out_up = jnp.dot(grad_up, proj_hidden[1].T, preferred_element_type=jnp.float32)
    in_down = jnp.dot(hidden, proj_hidden[2].T, preferred_element_type=jnp.float32)
    sketch = jnp.stack([pair_sketch(in_gate, out_gate), pair_sketch(in_up, out_up), pair_sketch(in_down, out_down)], axis=1)
    flat = sketch.reshape(NSEQ, 3 * K * K)
    scores = jnp.dot(flat, queries.astype(jnp.float32).T, precision=lax.Precision.HIGHEST)
    return (block_out, scores)
```

```python
import functools

import jax
import jax.numpy as jnp
from jax import lax
from jax.experimental import pallas as pl
from jax.experimental.pallas import tpu as pltpu
from jax.sharding import PartitionSpec as P

SEQ = 256


epsilon = 1e-06


def contract_last(left_mat, right_mat):
    return lax.dot_general(
        left_mat, right_mat, (((1,), (1,)), ((), ())), preferred_element_type=jnp.float32
    )


def contract_lead(left_mat, right_mat):
    return lax.dot_general(
        left_mat, right_mat, (((0,), (1,)), ((), ())), preferred_element_type=jnp.float32
    )


def pair_sketch(inputs_side, grads_side, seq_count):
    inputs_seq = inputs_side.reshape(seq_count, SEQ, inputs_side.shape[1])
    grads_seq = grads_side.reshape(seq_count, SEQ, grads_side.shape[1])
    return jnp.einsum("stk,stj->skj", inputs_seq, grads_seq, precision=lax.Precision.HIGHEST)


def on_device_plain(
    hidden_in, w_gate, w_up, w_down, norm_gain, out_cotangent, proj_model, proj_hidden, queries
):
    width_cols = hidden_in.shape[1]
    rank = proj_model.shape[1]
    devices = lax.axis_size("dp")
    width = width_cols * devices
    total_rows = hidden_in.shape[0]
    seq_count = total_rows // SEQ
    in_sides = proj_model[0:2].reshape(2 * rank, width)
    out_side = proj_model[2]
    first_col = lax.axis_index("dp") * width_cols
    piece = lax.all_gather(hidden_in, "dp", axis=1, tiled=True)
    gate_value = jnp.dot(piece, w_gate, preferred_element_type=jnp.float32)
    up_value = jnp.dot(piece, w_up, preferred_element_type=jnp.float32)
    projected = contract_last(piece, in_sides)
    in_gate = projected[:, :rank]
    in_up = projected[:, rank:]
    sigmoid_gate = jax.nn.sigmoid(gate_value)
    activated = gate_value * sigmoid_gate
    hidden = (activated * up_value).astype(jnp.bfloat16)
    down_cols = lax.psum_scatter(
        contract_lead(w_down, hidden), "dp", scatter_dimension=0, tiled=True
    )
    gain_cols = lax.dynamic_slice_in_dim(norm_gain, first_col, width_cols, 0)[:, None]
    scaled = gain_cols * jnp.transpose(out_cotangent).astype(jnp.float32)
    square_sums, mixed_sums = lax.psum(
        (jnp.sum(down_cols * down_cols, axis=0), jnp.sum(scaled * down_cols, axis=0)), "dp"
    )
    inv_rms = lax.rsqrt(square_sums / width + epsilon)[None, :]
    mixed_mean = (mixed_sums / width)[None, :]
    block_out = (
        hidden_in.astype(jnp.float32) + jnp.transpose(down_cols * inv_rms * gain_cols)
    ).astype(jnp.bfloat16)
    grad_cols = (inv_rms * (scaled - down_cols * inv_rms * inv_rms * mixed_mean)).astype(
        jnp.bfloat16
    )
    block_cols = lax.all_gather(grad_cols, "dp", axis=0, tiled=True)
    grad_hidden = contract_lead(block_cols, w_down)
    out_down = contract_lead(block_cols, out_side)
    grad_up = (grad_hidden * activated).astype(jnp.bfloat16)
    grad_gate = (
        grad_hidden * up_value * sigmoid_gate * (1.0 + gate_value * (1.0 - sigmoid_gate))
    ).astype(jnp.bfloat16)
    out_gate = contract_last(grad_gate, proj_hidden[0])
    out_up = contract_last(grad_up, proj_hidden[1])
    in_down = contract_last(hidden, proj_hidden[2])
    out_gate, out_up, in_down = lax.psum((out_gate, out_up, in_down), "dp")
    sketch = jnp.stack(
        [
            pair_sketch(in_gate, out_gate, seq_count),
            pair_sketch(in_up, out_up, seq_count),
            pair_sketch(in_down, out_down, seq_count),
        ],
        axis=1,
    )
    flat = sketch.reshape(seq_count, 3 * rank * rank)
    scores = jnp.dot(flat, queries.astype(jnp.float32).T, precision=lax.Precision.HIGHEST)
    return (block_out, scores)


CHUNKS = 2
BF = jnp.bfloat16
F32 = jnp.float32
HIGH = lax.Precision.HIGHEST


def matmul(a, b, precision=None):
    return lax.dot_general(
        a, b, (((1,), (0,)), ((), ())), precision=precision, preferred_element_type=F32
    )


def matmul_nt(a, b, precision=None):
    return lax.dot_general(
        a, b, (((1,), (1,)), ((), ())), precision=precision, preferred_element_type=F32
    )


def fused(
    n,
    x_in, cot_in, gain, w_gate, w_up, w_down, proj_model, proj_hidden, queries,
    out, scores,
    wg, wu, wd, pm, ph, qs,
    xa, ga, gate, up, gh, hid, ip_t, od, id_t,
    xch, xf, cf, ownf, prt, rsr, down, stats, osend, orecv, skp, rsk, skf, pairs,
    w_sem, m_sem, x_ssem, x_rsem, a_s, a_r, p_s, p_r, b_s, b_r, q_s, q_r,
    d_s, d_r, r_s, r_r, st_s, st_r, k_s, k_r, f_s, f_r,
):
    half = n // 2
    devices = 2 * n
    me = lax.axis_index("dp")
    chip, core = me // 2, lax.rem(me, 2)
    tokens = x_in.shape[0]
    narrow = x_in.shape[1]
    wide = 2 * narrow
    th = tokens // 2
    tc = th // CHUNKS
    width = wide * n
    seqs = tokens // SEQ
    rank = od.shape[1]
    rows_of = 3 * rank

    def chip_at(pos):
        pos = lax.rem(pos + 2 * n, n)
        return jnp.where(pos < half, 2 * pos, 2 * (n - 1 - pos) + 1)

    even = lax.rem(chip, 2) == 0
    here = jnp.where(even, chip // 2, n - 1 - chip // 2)
    right = chip_at(here + 1) * 2 + core
    left = chip_at(here - 1) * 2 + core
    partner = chip * 2 + 1 - core
    onward = (right, left)

    def cols(q):
        return pl.ds(pl.multiple_of(q * wide, 128), wide)

    def rows(whose, ch):
        return pl.ds(pl.multiple_of(whose * th + ch * tc, 16), tc)

    def half_rows(whose):
        return pl.ds(pl.multiple_of(whose * th, 16), th)

    def remote(src, dst, ssem, rsem, target):
        return pltpu.make_async_remote_copy(
            src_ref=src, dst_ref=dst, send_sem=ssem, recv_sem=rsem,
            device_id={"dp": target}, device_id_type=pl.DeviceIdType.MESH,
        )

    def weight_copy(which, q):
        span = pl.ds(pl.multiple_of(q * wide, 16), wide)
        src, dst = ((w_gate, wg), (w_up, wu))[which]
        return pltpu.make_async_copy(src.at[span, :], dst.at[span, :], w_sem.at[which, q])

    def block_chip(i):
        hop = (i + 1) // 2
        return jnp.where(lax.rem(i, 2) == 1, chip_at(here - hop), chip_at(here + hop))

    pm_copy = pltpu.make_async_copy(proj_model, pm, m_sem.at[0])
    ph_copy = pltpu.make_async_copy(proj_hidden, ph, m_sem.at[1])
    wd_copy = pltpu.make_async_copy(w_down, wd, m_sem.at[2])
    q_copy = pltpu.make_async_copy(queries, qs, m_sem.at[3])
    for which in range(2):
        weight_copy(which, chip).start()
    pm_copy.start()

    @pl.loop(1, n)
    def _(i):
        for which in range(2):
            weight_copy(which, block_chip(i)).start()

    wd_copy.start()
    ph_copy.start()
    q_copy.start()

    barrier = pltpu.get_barrier_semaphore()

    @pl.loop(1, devices)
    def _(o):
        pl.semaphore_signal(
            barrier, inc=1, device_id={"dp": lax.rem(me + o, devices)},
            device_id_type=pl.DeviceIdType.MESH,
        )

    pl.semaphore_wait(barrier, devices - 1)

    trades = []
    for at, ref in enumerate((x_in, cot_in)):
        trades.append(
            remote(ref.at[half_rows(1 - core), :], xch.at[at], x_ssem.at[at], x_rsem.at[at], partner)
        )
        trades[-1].start()
    for ref in (gate, up, gh, ip_t, od, skp):
        ref[...] = jnp.zeros_like(ref)

    def join(at, ref, dst):
        trades[at].wait_recv()
        mine = ref[half_rows(core), :].astype(F32)
        theirs = xch[at].astype(F32)

        @pl.when(core == 0)
        def _():
            dst[:, :narrow] = mine
            dst[:, narrow:] = theirs

        @pl.when(core == 1)
        def _():
            dst[:, :narrow] = theirs
            dst[:, narrow:] = mine

    join(0, x_in, xf)
    xa[half_rows(core), cols(chip)] = xf[...].astype(BF)

    def gather(buf, ssem, rsem, psend, precv, compute, before_loop):
        def hop(direction, at, ch, q):
            ref = buf.at[rows(core, ch), cols(q)]
            where = (direction, at, ch)
            return remote(ref, ref, ssem.at[where], rsem.at[where], onward[direction])

        def last_hop(direction, ch, q):
            ref = buf.at[rows(core, ch), cols(q)]
            return remote(
                ref, ref, ssem.at[0, half, ch], rsem.at[0, half, ch], onward[direction]
            )

        def share(direction, at, ch, q, whose):
            ref = buf.at[rows(whose, ch), cols(q)]
            where = (direction, at, ch)
            return remote(ref, ref, psend.at[where], precv.at[where], partner)

        for ch in range(CHUNKS):
            for direction in range(2):
                hop(direction, 1, ch, chip).start()
        for ch in range(CHUNKS):
            share(0, 0, ch, chip, core).start()
        before_loop()
        for ch in range(CHUNKS):
            share(0, 0, ch, chip, 1 - core).wait_recv()
        compute(chip)

        @pl.loop(1, n)
        def _(i):
            at = (i + 1) // 2
            odd = lax.rem(i, 2) == 1

            @pl.when(odd & (at < half))
            def _():
                for ch in range(CHUNKS):
                    for direction in range(2):
                        q = chip_at(here - at) if direction == 0 else chip_at(here + at)
                        hop(direction, at, ch, q).wait_recv()

                        @pl.when(at < half - 1)
                        def _():
                            hop(direction, at + 1, ch, q).start()

                        @pl.when((at == half - 1) & (core == direction))
                        def _():
                            last_hop(direction, ch, q).start()

                        share(direction, at, ch, q, core).start()

            @pl.when(i == n - 1)
            def _():
                q = chip_at(here - half)
                for ch in range(CHUNKS):
                    last_hop(0, ch, q).wait_recv()
                    share(0, half, ch, q, core).start()

            q = block_chip(i)
            for ch in range(CHUNKS):
                share(1 - lax.rem(i, 2), at, ch, q, 1 - core).wait_recv()
            compute(q)

        def drain():
            for ch in range(CHUNKS):
                share(0, 0, ch, chip, core).wait_send()
                for direction in range(2):
                    for at in range(1, half):
                        back = at - 1 if direction == 0 else 1 - at
                        hop(direction, at, ch, chip_at(here - back)).wait_send()
                        share(direction, at, ch, chip, core).wait_send()
                last_hop(0, ch, chip).wait_send()
                share(0, half, ch, chip, core).wait_send()

        return drain

    def forward(q):
        for which in range(2):
            weight_copy(which, q).wait()
        block = xa[:, cols(q)]
        span = pl.ds(pl.multiple_of(q * wide, 16), wide)
        gate[...] += matmul(block, wg[span, :])
        up[...] += matmul(block, wu[span, :])
        ip_t[...] += matmul_nt(pm[: 2 * rank, cols(q)], block)

    def first_prep():
        join(1, cot_in, cf)
        pm_copy.wait()

    drain = gather(xa, a_s, a_r, p_s, p_r, forward, first_prep)

    piece = 64

    @pl.loop(0, tokens // piece)
    def _(i):
        span = pl.ds(pl.multiple_of(i * piece, 16), piece)
        g = gate[span, :]
        u = up[span, :]
        s = jax.nn.sigmoid(g)
        act = g * s
        hid[span, :] = (act * u).astype(BF)
        gate[span, :] = act
        up[span, :] = u * s * (1.0 + g * (1.0 - s))

    drain()
    wd_copy.wait()

    def dest(j):
        far = half - (j + 1) // 2
        away = jnp.where(lax.rem(j, 2) == 1, far, -far)
        return jnp.where(
            j == 0, chip_at(here + half), jnp.where(j == n - 1, chip, chip_at(here + away))
        )

    def part_copy(j, q):
        return remote(
            xa.at[half_rows(1 - core), cols(q)], prt.at[j], d_s.at[j], d_r.at[j], partner
        )

    def part(j):
        q = dest(j)
        xa[half_rows(1 - core), cols(q)] = matmul(
            hid[half_rows(1 - core), :], wd[:, cols(q)]
        ).astype(BF)
        part_copy(j, q).start()
        ownf[lax.rem(j, 2)] = matmul(hid[half_rows(core), :], wd[:, cols(q)])

    def ring_sum(direction, step, ch, q):
        return remote(
            xa.at[rows(core, ch), cols(q)],
            rsr.at[direction, step, pl.ds(ch * tc, tc), :],
            r_s.at[direction, step, ch],
            r_r.at[direction, step, ch],
            onward[direction],
        )

    def own_sum(j, ch):
        span = pl.ds(ch * tc, tc)
        return ownf[lax.rem(j, 2), span, :] + prt[j, span, :].astype(F32)

    def finish(j):
        q = dest(j)
        part_copy(j, q).wait_recv()

        @pl.when(j == 0)
        def _():
            for ch in range(CHUNKS):
                xa[rows(core, ch), cols(q)] = own_sum(j, ch).astype(BF)
                for direction in range(2):

                    @pl.when(core == direction)
                    def _():
                        ring_sum(direction, 0, ch, q).start()

        step = (j + 1) // 2
        for direction in range(2):

            @pl.when((j > 0) & (lax.rem(j, 2) == 1 - direction))
            def _():
                for ch in range(CHUNKS):
                    span = pl.ds(ch * tc, tc)
                    carried = (step > 1) | (core == direction)

                    @pl.when(carried)
                    def _():
                        ring_sum(direction, step - 1, ch, q).wait_recv()
                        xa[rows(core, ch), cols(q)] = (
                            own_sum(j, ch) + rsr[direction, step - 1, span, :].astype(F32)
                        ).astype(BF)

                    @pl.when(jnp.logical_not(carried))
                    def _():
                        xa[rows(core, ch), cols(q)] = own_sum(j, ch).astype(BF)

                    ring_sum(direction, step, ch, q).start()

    part(0)

    @pl.loop(1, n)
    def _(j):
        part(j)
        finish(j - 1)

    part_copy(n - 1, chip).wait_recv()
    for ch in range(CHUNKS):
        span = pl.ds(ch * tc, tc)
        for direction in range(2):
            ring_sum(direction, half - 1, ch, chip).wait_recv()
        down[span, :] = (
            own_sum(n - 1, ch)
            + rsr[0, half - 1, span, :].astype(F32)
            + rsr[1, half - 1, span, :].astype(F32)
        )

    gains = gain[:, cols(chip)]
    ones = jnp.ones((8, 128), F32)

    def fold(v):
        total = v[:, :128]
        for at in range(128, wide, 128):
            total = total + v[:, at : at + 128]
        return matmul_nt(ones, total, HIGH)

    stats[chip, 0:8, :] = fold(down[...] * down[...])
    stats[chip, 8:16, :] = fold(gains * cf[...] * down[...])

    def stat_copy(o):
        other = lax.rem(chip + o, n)
        ref = stats.at[chip]
        return remote(ref, ref, st_s.at[o], st_r.at[o], other * 2 + core)

    def stat_recv(o):
        ref = stats.at[lax.rem(chip + n - o, n)]
        return remote(ref, ref, st_s.at[o], st_r.at[o], partner)

    for o in range(1, n):
        stat_copy(o).start()
    for o in range(1, n):
        stat_recv(o).wait_recv()
    total = stats[0]
    for at in range(1, n):
        total = total + stats[at]
    inv_row = lax.rsqrt(total[0:8] / width + epsilon)
    mean_row = total[8:16] / width
    turned = jnp.transpose(jnp.concatenate([inv_row] * 8 + [mean_row] * 8, axis=0))
    inv_rms = turned[:, 0:1]
    mixed_mean = turned[:, 64:65]
    normed = down[...] * inv_rms
    ga[half_rows(core), cols(chip)] = (
        inv_rms * (gains * cf[...] - normed * (inv_rms * mixed_mean))
    ).astype(BF)
    xf[...] = xf[...] + normed * gains

    out_copy = remote(osend, orecv, m_sem.at[4], m_sem.at[5], partner)

    def block_output():
        @pl.when(core == 0)
        def _():
            osend[...] = xf[:, narrow:].astype(BF)
            out[half_rows(0), :] = xf[:, :narrow].astype(BF)

        @pl.when(core == 1)
        def _():
            osend[...] = xf[:, :narrow].astype(BF)
            out[half_rows(1), :] = xf[:, narrow:].astype(BF)

        out_copy.start()
        ph_copy.wait()
        id_t[...] = matmul_nt(ph[2 * rank :, :], hid[...])

    def backward(q):
        block = ga[:, cols(q)]
        gh[...] += matmul_nt(block, wd[:, cols(q)])
        od[...] += matmul_nt(block, pm[2 * rank :, cols(q)])

    drain = gather(ga, b_s, b_r, q_s, q_r, backward, block_output)

    for s in range(seqs):
        span = pl.ds(s * SEQ, SEQ)
        lanes = slice(s * SEQ, (s + 1) * SEQ)
        back = gh[span, :]
        out_gate = matmul_nt((back * up[span, :]).astype(BF), ph[:rank, :])
        out_up = matmul_nt((back * gate[span, :]).astype(BF), ph[rank : 2 * rank, :])
        first = s * rows_of
        skp[first : first + rank, :rank] = matmul(ip_t[:rank, lanes], out_gate, HIGH)
        skp[first + rank : first + 2 * rank, :rank] = matmul(ip_t[rank:, lanes], out_up, HIGH)
        skp[first + 2 * rank : first + 3 * rank, :rank] = matmul(
            id_t[:, lanes], od[span, :], HIGH
        )

    share = seqs * rows_of // devices

    def share_rows(d):
        return pl.ds(pl.multiple_of(d * share, 8), share)

    def scatter(o):
        to = lax.rem(me + o, devices)
        return remote(skp.at[share_rows(to), :], rsk.at[o], k_s.at[o], k_r.at[o], to)

    @pl.loop(1, devices)
    def _(o):
        scatter(o).start()

    rsk[0] = skp[share_rows(me), :]

    @pl.loop(1, devices)
    def _(o):
        scatter(o).wait_recv()

    summed = rsk[0]
    for o in range(1, devices):
        summed = summed + rsk[o]
    skf[share_rows(me), :] = summed

    def spread(o):
        ref = skf.at[share_rows(me), :]
        return remote(ref, ref, f_s.at[o], f_r.at[o], lax.rem(me + o, devices))

    def spread_recv(o):
        ref = skf.at[share_rows(lax.rem(me + devices - o, devices)), :]
        return remote(ref, ref, f_s.at[o], f_r.at[o], partner)

    @pl.loop(1, devices)
    def _(o):
        spread(o).start()

    out_copy.wait_recv()
    for k in range(2):

        @pl.when(core == k)
        def _():
            out[half_rows(1 - k), :] = orecv[...]

    drain()
    out_copy.wait_send()
    for trade in trades:
        trade.wait_send()
    for j in range(n):
        part_copy(j, chip).wait_send()
    for ch in range(CHUNKS):
        for direction in range(2):
            for step in range(1, half):
                ring_sum(direction, step, ch, chip).wait_send()

            @pl.when(core == direction)
            def _():
                ring_sum(direction, 0, ch, chip).wait_send()

    for o in range(1, n):
        stat_copy(o).wait_send()

    @pl.loop(1, devices)
    def _(o):
        scatter(o).wait_send()

    q_copy.wait()

    @pl.loop(1, devices)
    def _(o):
        spread_recv(o).wait_recv()

    count = seqs * rows_of // 2
    pairs[:, :rank] = skf[pl.ds(0, count, stride=2), :][:, :rank]
    pairs[:, rank:] = skf[pl.ds(1, count, stride=2), :][:, :rank]
    tiles = rows_of // 2

    def add(t, sums):
        tile = qs[:, pl.ds(pl.multiple_of(t * 2 * rank, 128), 2 * rank)].astype(F32)
        return tuple(
            sums[s] + tile * pairs[pl.ds(s * tiles + t, 1), :] for s in range(seqs)
        )

    zero = jnp.zeros((qs.shape[0], 2 * rank), F32)
    sums = lax.fori_loop(0, tiles, add, (zero,) * seqs)
    for s in range(seqs):
        scores[s : s + 1, :] = matmul_nt(ones, sums[s], HIGH)[0:1, :]

    @pl.loop(1, devices)
    def _(o):
        spread(o).wait_send()


def fused_fits(hidden_in, proj_model, queries, devices):
    n = devices // 2
    tokens, narrow = hidden_in.shape
    rank = proj_model.shape[1]
    rows_of = tokens // SEQ * 3 * rank
    return (
        devices % 4 == 0
        and n >= 4
        and (2 * narrow) % 128 == 0
        and rank == 64
        and tokens % (SEQ * 2) == 0
        and rows_of % (8 * devices) == 0
    )


def on_device_fused(
    hidden_in, w_gate, w_up, w_down, norm_gain, out_cotangent, proj_model, proj_hidden, queries
):
    devices = lax.axis_size("dp")
    n = devices // 2
    half = n // 2
    tokens, narrow = hidden_in.shape
    wide, th = 2 * narrow, tokens // 2
    width, units = w_gate.shape
    rank = proj_model.shape[1]
    seqs = tokens // SEQ
    sk_rows = seqs * 3 * rank
    vmem = pltpu.VMEM
    dma = pltpu.SemaphoreType.DMA
    block = (th, wide)
    scratch = [
        vmem((width, units), BF), vmem((width, units), BF), vmem((units, width), BF),
        vmem((3 * rank, width), BF), vmem((3 * rank, units), BF), vmem(queries.shape, BF),
        vmem((tokens, width), BF), vmem((tokens, width), BF),
        vmem((tokens, units), F32), vmem((tokens, units), F32), vmem((tokens, units), F32),
        vmem((tokens, units), BF), vmem((2 * rank, tokens), F32), vmem((tokens, rank), F32),
        vmem((rank, tokens), F32),
        vmem((2, th, narrow), BF), vmem(block, F32), vmem(block, F32),
        vmem((2,) + block, F32), vmem((n,) + block, BF), vmem((2, half) + block, BF),
        vmem(block, F32), vmem((n, 16, th), F32),
        vmem((th, narrow), BF), vmem((th, narrow), BF),
        vmem((sk_rows, 128), F32), vmem((devices, sk_rows // devices, 128), F32),
        vmem((sk_rows, 128), F32), vmem((sk_rows // 2, 2 * rank), F32),
        dma((2, n)), dma((6,)), dma((2,)), dma((2,)),
    ]
    scratch += [dma((2, half + 1, CHUNKS))] * 8
    scratch += [dma((n,))] * 2 + [dma((2, half, CHUNKS))] * 2 + [dma((n,))] * 2
    scratch += [dma((devices,))] * 4
    near = pl.BlockSpec(memory_space=pltpu.VMEM)
    far = pl.BlockSpec(memory_space=pl.ANY)
    return pl.pallas_call(
        functools.partial(fused, n),
        out_shape=(
            jax.ShapeDtypeStruct((tokens, narrow), BF),
            jax.ShapeDtypeStruct((seqs, queries.shape[0]), F32),
        ),
        in_specs=[near, near, near] + [far] * 6,
        out_specs=(near, near),
        scratch_shapes=scratch,
        compiler_params=pltpu.CompilerParams(
            collective_id=0, has_side_effects=True, vmem_limit_bytes=VMEM_LIMIT
        ),
    )(
        hidden_in, out_cotangent, norm_gain[None, :], w_gate, w_up, w_down,
        proj_model.reshape(3 * rank, width), proj_hidden.reshape(3 * rank, units), queries,
    )


VMEM_LIMIT = 63 * 1024 * 1024


def on_device(hidden_in, w_gate, w_up, w_down, norm_gain, out_cotangent, proj_model, *rest):
    form = on_device_plain
    if fused_fits(hidden_in, proj_model, rest[1], lax.axis_size("dp")):
        form = on_device_fused
    return form(
        hidden_in, w_gate, w_up, w_down, norm_gain, out_cotangent, proj_model, *rest
    )


def solution(mesh):
    in_specs = (
        P("group", "dp"),
        P(None, "dp"),
        P(None, "dp"),
        P("dp", None),
        P(),
        P("group", "dp"),
        P(),
        P(None, None, "dp"),
        P("dp", None),
    )
    out_specs = (P("group", "dp"), P("group", "dp"))
    return jax.shard_map(
        on_device, mesh=mesh, in_specs=in_specs, out_specs=out_specs, check_vma=False
    )
```

```python
import functools

import jax
import jax.numpy as jnp
from jax import lax
from jax.experimental import pallas as pl
from jax.experimental.pallas import tpu as pltpu
from jax.sharding import PartitionSpec as P

SEQ = 256


epsilon = 1e-06


def contract_last(left_mat, right_mat):
    return lax.dot_general(
        left_mat, right_mat, (((1,), (1,)), ((), ())), preferred_element_type=jnp.float32
    )


def contract_lead(left_mat, right_mat):
    return lax.dot_general(
        left_mat, right_mat, (((0,), (1,)), ((), ())), preferred_element_type=jnp.float32
    )


def pair_sketch(inputs_side, grads_side, seq_count):
    inputs_seq = inputs_side.reshape(seq_count, SEQ, inputs_side.shape[1])
    grads_seq = grads_side.reshape(seq_count, SEQ, grads_side.shape[1])
    return jnp.einsum("stk,stj->skj", inputs_seq, grads_seq, precision=lax.Precision.HIGHEST)


def on_device_plain(
    hidden_in, w_gate, w_up, w_down, norm_gain, out_cotangent, proj_model, proj_hidden, queries
):
    width_cols = hidden_in.shape[1]
    rank = proj_model.shape[1]
    devices = lax.axis_size("dp")
    width = width_cols * devices
    total_rows = hidden_in.shape[0]
    seq_count = total_rows // SEQ
    in_sides = proj_model[0:2].reshape(2 * rank, width)
    out_side = proj_model[2]
    first_col = lax.axis_index("dp") * width_cols
    piece = lax.all_gather(hidden_in, "dp", axis=1, tiled=True)
    gate_value = jnp.dot(piece, w_gate, preferred_element_type=jnp.float32)
    up_value = jnp.dot(piece, w_up, preferred_element_type=jnp.float32)
    projected = contract_last(piece, in_sides)
    in_gate = projected[:, :rank]
    in_up = projected[:, rank:]
    sigmoid_gate = jax.nn.sigmoid(gate_value)
    activated = gate_value * sigmoid_gate
    hidden = (activated * up_value).astype(jnp.bfloat16)
    down_cols = lax.psum_scatter(
        contract_lead(w_down, hidden), "dp", scatter_dimension=0, tiled=True
    )
    gain_cols = lax.dynamic_slice_in_dim(norm_gain, first_col, width_cols, 0)[:, None]
    scaled = gain_cols * jnp.transpose(out_cotangent).astype(jnp.float32)
    square_sums, mixed_sums = lax.psum(
        (jnp.sum(down_cols * down_cols, axis=0), jnp.sum(scaled * down_cols, axis=0)), "dp"
    )
    inv_rms = lax.rsqrt(square_sums / width + epsilon)[None, :]
    mixed_mean = (mixed_sums / width)[None, :]
    block_out = (
        hidden_in.astype(jnp.float32) + jnp.transpose(down_cols * inv_rms * gain_cols)
    ).astype(jnp.bfloat16)
    grad_cols = (inv_rms * (scaled - down_cols * inv_rms * inv_rms * mixed_mean)).astype(
        jnp.bfloat16
    )
    block_cols = lax.all_gather(grad_cols, "dp", axis=0, tiled=True)
    grad_hidden = contract_lead(block_cols, w_down)
    out_down = contract_lead(block_cols, out_side)
    grad_up = (grad_hidden * activated).astype(jnp.bfloat16)
    grad_gate = (
        grad_hidden * up_value * sigmoid_gate * (1.0 + gate_value * (1.0 - sigmoid_gate))
    ).astype(jnp.bfloat16)
    out_gate = contract_last(grad_gate, proj_hidden[0])
    out_up = contract_last(grad_up, proj_hidden[1])
    in_down = contract_last(hidden, proj_hidden[2])
    out_gate, out_up, in_down = lax.psum((out_gate, out_up, in_down), "dp")
    sketch = jnp.stack(
        [
            pair_sketch(in_gate, out_gate, seq_count),
            pair_sketch(in_up, out_up, seq_count),
            pair_sketch(in_down, out_down, seq_count),
        ],
        axis=1,
    )
    flat = sketch.reshape(seq_count, 3 * rank * rank)
    scores = jnp.dot(flat, queries.astype(jnp.float32).T, precision=lax.Precision.HIGHEST)
    return (block_out, scores)


CHUNKS = 2
BF = jnp.bfloat16
F32 = jnp.float32
HIGH = lax.Precision.HIGHEST


def matmul(a, b, precision=None):
    return lax.dot_general(
        a, b, (((1,), (0,)), ((), ())), precision=precision, preferred_element_type=F32
    )


def matmul_nt(a, b, precision=None):
    return lax.dot_general(
        a, b, (((1,), (1,)), ((), ())), precision=precision, preferred_element_type=F32
    )


def matmul_tn(a, b):
    return lax.dot_general(a, b, (((0,), (0,)), ((), ())), preferred_element_type=F32)


def fused(
    n,
    x_in, cot_in, gain, w_gate, w_up, w_down, proj_model, proj_hidden, queries,
    out, scores,
    wg, wu, wd, pm, ph, qs,
    xa, ga, gate, up, gh, hid, ip_t, od_t, id_t,
    xch, xf, cf, gcol, ownf, prt, rsr, down, stats, osend, orecv, skp, rsk, skf, pairs,
    w_sem, m_sem, x_ssem, x_rsem, a_s, a_r, p_s, p_r, b_s, b_r, q_s, q_r,
    d_s, d_r, r_s, r_r, st_s, st_r, k_s, k_r, f_s, f_r,
):
    half = n // 2
    devices = 2 * n
    me = lax.axis_index("dp")
    chip, core = me // 2, lax.rem(me, 2)
    narrow, tokens = x_in.shape
    wide = 2 * narrow
    th = tokens // 2
    fc = wide // CHUNKS
    width = wide * n
    seqs = tokens // SEQ
    rank = od_t.shape[0]
    rows_of = 3 * rank

    def chip_at(pos):
        pos = lax.rem(pos + 2 * n, n)
        return jnp.where(pos < half, 2 * pos, 2 * (n - 1 - pos) + 1)

    even = lax.rem(chip, 2) == 0
    here = jnp.where(even, chip // 2, n - 1 - chip // 2)
    right = chip_at(here + 1) * 2 + core
    left = chip_at(here - 1) * 2 + core
    partner = chip * 2 + 1 - core
    onward = (right, left)

    def cols(q):
        return pl.ds(pl.multiple_of(q * wide, 128), wide)

    def feats(q, ch):
        return pl.ds(pl.multiple_of(q * wide + ch * fc, 16), fc)

    def all_feats(q):
        return pl.ds(pl.multiple_of(q * wide, 16), wide)

    def lanes(whose):
        return pl.ds(pl.multiple_of(whose * th, 128), th)

    def remote(src, dst, ssem, rsem, target):
        return pltpu.make_async_remote_copy(
            src_ref=src, dst_ref=dst, send_sem=ssem, recv_sem=rsem,
            device_id={"dp": target}, device_id_type=pl.DeviceIdType.MESH,
        )

    def weight_copy(which, q):
        src, dst = ((w_gate, wg), (w_up, wu))[which]
        return pltpu.make_async_copy(src.at[:, cols(q)], dst.at[:, cols(q)], w_sem.at[which, q])

    def block_chip(i):
        hop = (i + 1) // 2
        return jnp.where(lax.rem(i, 2) == 1, chip_at(here - hop), chip_at(here + hop))

    pm_copy = pltpu.make_async_copy(proj_model, pm, m_sem.at[0])
    ph_copy = pltpu.make_async_copy(proj_hidden, ph, m_sem.at[1])
    wd_copy = pltpu.make_async_copy(w_down, wd, m_sem.at[2])
    q_copy = pltpu.make_async_copy(queries, qs, m_sem.at[3])
    for which in range(2):
        weight_copy(which, chip).start()
    pm_copy.start()

    @pl.loop(1, n)
    def _(i):
        for which in range(2):
            weight_copy(which, block_chip(i)).start()

    wd_copy.start()
    ph_copy.start()
    q_copy.start()

    barrier = pltpu.get_barrier_semaphore()

    @pl.loop(1, devices)
    def _(o):
        pl.semaphore_signal(
            barrier, inc=1, device_id={"dp": lax.rem(me + o, devices)},
            device_id_type=pl.DeviceIdType.MESH,
        )

    pl.semaphore_wait(barrier, devices - 1)

    trades = []
    for at, ref in enumerate((x_in, cot_in)):
        trades.append(
            remote(ref.at[:, lanes(1 - core)], xch.at[at], x_ssem.at[at], x_rsem.at[at], partner)
        )
        trades[-1].start()
    for ref in (gate, up, gh, ip_t, od_t, skp):
        ref[...] = jnp.zeros_like(ref)

    def join(at, ref, dst):
        trades[at].wait_recv()
        dst[own_feats, :] = ref[:, lanes(core)].astype(F32)
        dst[other_feats, :] = xch[at].astype(F32)

    own_feats = pl.ds(pl.multiple_of(core * narrow, 16), narrow)
    other_feats = pl.ds(pl.multiple_of((1 - core) * narrow, 16), narrow)
    join(0, x_in, xf)
    xa[all_feats(chip), lanes(core)] = xf[...].astype(BF)

    def gather(buf, ssem, rsem, psend, precv, compute, before_loop):
        def hop(direction, at, ch, q):
            ref = buf.at[feats(q, ch), lanes(core)]
            where = (direction, at, ch)
            return remote(ref, ref, ssem.at[where], rsem.at[where], onward[direction])

        def last_hop(direction, ch, q):
            ref = buf.at[feats(q, ch), lanes(core)]
            return remote(
                ref, ref, ssem.at[0, half, ch], rsem.at[0, half, ch], onward[direction]
            )

        def share(direction, at, ch, q, whose):
            ref = buf.at[feats(q, ch), lanes(whose)]
            where = (direction, at, ch)
            return remote(ref, ref, psend.at[where], precv.at[where], partner)

        for ch in range(CHUNKS):
            for direction in range(2):
                hop(direction, 1, ch, chip).start()
        for ch in range(CHUNKS):
            share(0, 0, ch, chip, core).start()
        before_loop()
        for ch in range(CHUNKS):
            share(0, 0, ch, chip, 1 - core).wait_recv()
        compute(chip)

        @pl.loop(1, n)
        def _(i):
            at = (i + 1) // 2
            odd = lax.rem(i, 2) == 1

            @pl.when(odd & (at < half))
            def _():
                for ch in range(CHUNKS):
                    for direction in range(2):
                        q = chip_at(here - at) if direction == 0 else chip_at(here + at)
                        hop(direction, at, ch, q).wait_recv()

                        @pl.when(at < half - 1)
                        def _():
                            hop(direction, at + 1, ch, q).start()

                        @pl.when((at == half - 1) & (core == direction))
                        def _():
                            last_hop(direction, ch, q).start()

                        share(direction, at, ch, q, core).start()

            @pl.when(i == n - 1)
            def _():
                q = chip_at(here - half)
                for ch in range(CHUNKS):
                    last_hop(0, ch, q).wait_recv()
                    share(0, half, ch, q, core).start()

            q = block_chip(i)
            for ch in range(CHUNKS):
                share(1 - lax.rem(i, 2), at, ch, q, 1 - core).wait_recv()
            compute(q)

        def drain():
            for ch in range(CHUNKS):
                share(0, 0, ch, chip, core).wait_send()
                for direction in range(2):
                    for at in range(1, half):
                        back = at - 1 if direction == 0 else 1 - at
                        hop(direction, at, ch, chip_at(here - back)).wait_send()
                        share(direction, at, ch, chip, core).wait_send()
                last_hop(0, ch, chip).wait_send()
                share(0, half, ch, chip, core).wait_send()

        return drain

    def forward(q):
        for which in range(2):
            weight_copy(which, q).wait()
        block = xa[all_feats(q), :]
        gate[...] += matmul(wg[:, cols(q)], block)
        up[...] += matmul(wu[:, cols(q)], block)
        ip_t[...] += matmul(pm[: 2 * rank, cols(q)], block)

    def first_prep():
        join(1, cot_in, cf)
        gcol[...] = jnp.transpose(jnp.broadcast_to(gain[:, cols(chip)], (128, wide)))
        cf[...] = gcol[:, 0:1] * cf[...]
        pm_copy.wait()

    drain = gather(xa, a_s, a_r, p_s, p_r, forward, first_prep)

    piece = 32

    @pl.loop(0, gate.shape[0] // piece)
    def _(i):
        span = pl.ds(pl.multiple_of(i * piece, 16), piece)
        g = gate[span, :]
        u = up[span, :]
        s = jax.nn.sigmoid(g)
        act = g * s
        hid[span, :] = (act * u).astype(BF)
        gate[span, :] = act
        up[span, :] = u * s * (1.0 + g * (1.0 - s))

    drain()
    wd_copy.wait()

    def dest(j):
        far = half - (j + 1) // 2
        away = jnp.where(lax.rem(j, 2) == 1, far, -far)
        return jnp.where(
            j == 0, chip_at(here + half), jnp.where(j == n - 1, chip, chip_at(here + away))
        )

    def part_copy(j, q):
        return remote(
            xa.at[all_feats(q), lanes(1 - core)], prt.at[j], d_s.at[j], d_r.at[j], partner
        )

    def part(j):
        q = dest(j)
        slot = lax.rem(j, 2)
        ownf[slot] = matmul_tn(wd[:, cols(q)], hid[...])
        xa[all_feats(q), lanes(1 - core)] = ownf[slot, :, lanes(1 - core)].astype(BF)
        part_copy(j, q).start()

    def ring_sum(direction, step, ch, q):
        return remote(
            xa.at[feats(q, ch), lanes(core)],
            rsr.at[direction, step, pl.ds(ch * fc, fc), :],
            r_s.at[direction, step, ch],
            r_r.at[direction, step, ch],
            onward[direction],
        )

    def own_sum(j, ch):
        span = pl.ds(ch * fc, fc)
        return ownf[lax.rem(j, 2), span, lanes(core)] + prt[j, span, :].astype(F32)

    def finish(j):
        q = dest(j)
        part_copy(j, q).wait_recv()

        @pl.when(j == 0)
        def _():
            for ch in range(CHUNKS):
                xa[feats(q, ch), lanes(core)] = own_sum(j, ch).astype(BF)
                for direction in range(2):

                    @pl.when(core == direction)
                    def _():
                        ring_sum(direction, 0, ch, q).start()

        step = (j + 1) // 2
        for direction in range(2):

            @pl.when((j > 0) & (lax.rem(j, 2) == 1 - direction))
            def _():
                for ch in range(CHUNKS):
                    span = pl.ds(ch * fc, fc)
                    carried = (step > 1) | (core == direction)

                    @pl.when(carried)
                    def _():
                        ring_sum(direction, step - 1, ch, q).wait_recv()
                        xa[feats(q, ch), lanes(core)] = (
                            own_sum(j, ch) + rsr[direction, step - 1, span, :].astype(F32)
                        ).astype(BF)

                    @pl.when(jnp.logical_not(carried))
                    def _():
                        xa[feats(q, ch), lanes(core)] = own_sum(j, ch).astype(BF)

                    ring_sum(direction, step, ch, q).start()

    part(0)

    @pl.loop(1, n)
    def _(j):
        part(j)
        finish(j - 1)

    part_copy(n - 1, chip).wait_recv()
    for ch in range(CHUNKS):
        span = pl.ds(ch * fc, fc)
        for direction in range(2):
            ring_sum(direction, half - 1, ch, chip).wait_recv()
        down[span, :] = (
            own_sum(n - 1, ch)
            + rsr[0, half - 1, span, :].astype(F32)
            + rsr[1, half - 1, span, :].astype(F32)
        )

    def fold(v):
        return jnp.sum(v, axis=0, keepdims=True)

    stats[chip] = jnp.concatenate(
        [fold(down[...] * down[...]), fold(cf[...] * down[...]), jnp.zeros((6, th), F32)], axis=0
    )

    def stat_copy(o):
        other = lax.rem(chip + o, n)
        ref = stats.at[chip]
        return remote(ref, ref, st_s.at[o], st_r.at[o], other * 2 + core)

    def stat_recv(o):
        ref = stats.at[lax.rem(chip + n - o, n)]
        return remote(ref, ref, st_s.at[o], st_r.at[o], partner)

    for o in range(1, n):
        stat_copy(o).start()
    for o in range(1, n):
        stat_recv(o).wait_recv()
    total = stats[0]
    for at in range(1, n):
        total = total + stats[at]
    inv_rms = lax.rsqrt(total[0:1] / width + epsilon)
    mixed_mean = total[1:2] / width
    normed = down[...] * inv_rms
    ga[all_feats(chip), lanes(core)] = (
        inv_rms * (cf[...] - normed * (inv_rms * mixed_mean))
    ).astype(BF)

    out_copy = remote(osend, orecv, m_sem.at[4], m_sem.at[5], partner)

    def block_output():
        xf[...] = xf[...] + down[...] * inv_rms * gcol[:, 0:1]
        osend[...] = xf[other_feats, :].astype(BF)
        out_copy.start()
        out[:, lanes(core)] = xf[own_feats, :].astype(BF)
        ph_copy.wait()
        id_t[...] = matmul(ph[2 * rank :, :], hid[...])

    def backward(q):
        block = ga[all_feats(q), :]
        gh[...] += matmul(wd[:, cols(q)], block)
        od_t[...] += matmul(pm[2 * rank :, cols(q)], block)

    drain = gather(ga, b_s, b_r, q_s, q_r, backward, block_output)

    out_gate = matmul(ph[:rank, :], (gh[...] * up[...]).astype(BF))
    out_up = matmul(ph[rank : 2 * rank, :], (gh[...] * gate[...]).astype(BF))
    for s in range(seqs):
        at = slice(s * SEQ, (s + 1) * SEQ)
        first = s * rows_of
        skp[first : first + rank, :rank] = matmul_nt(ip_t[:rank, at], out_gate[:, at], HIGH)
        skp[first + rank : first + 2 * rank, :rank] = matmul_nt(
            ip_t[rank:, at], out_up[:, at], HIGH
        )
        skp[first + 2 * rank : first + 3 * rank, :rank] = matmul_nt(
            id_t[:, at], od_t[:, at], HIGH
        )

    share = seqs * rows_of // devices

    def share_rows(d):
        return pl.ds(pl.multiple_of(d * share, 8), share)

    def scatter(o):
        to = lax.rem(me + o, devices)
        return remote(skp.at[share_rows(to), :], rsk.at[o], k_s.at[o], k_r.at[o], to)

    @pl.loop(1, devices)
    def _(o):
        scatter(o).start()

    rsk[0] = skp[share_rows(me), :]

    @pl.loop(1, devices)
    def _(o):
        scatter(o).wait_recv()

    summed = rsk[0]
    for o in range(1, devices):
        summed = summed + rsk[o]
    skf[share_rows(me), :] = summed

    def spread(o):
        ref = skf.at[share_rows(me), :]
        return remote(ref, ref, f_s.at[o], f_r.at[o], lax.rem(me + o, devices))

    def spread_recv(o):
        ref = skf.at[share_rows(lax.rem(me + devices - o, devices)), :]
        return remote(ref, ref, f_s.at[o], f_r.at[o], partner)

    @pl.loop(1, devices)
    def _(o):
        spread(o).start()

    out_copy.wait_recv()
    out[:, lanes(1 - core)] = orecv[...]

    drain()
    out_copy.wait_send()
    for trade in trades:
        trade.wait_send()
    for j in range(n):
        part_copy(j, chip).wait_send()
    for ch in range(CHUNKS):
        for direction in range(2):
            for step in range(1, half):
                ring_sum(direction, step, ch, chip).wait_send()

            @pl.when(core == direction)
            def _():
                ring_sum(direction, 0, ch, chip).wait_send()

    for o in range(1, n):
        stat_copy(o).wait_send()

    @pl.loop(1, devices)
    def _(o):
        scatter(o).wait_send()

    q_copy.wait()

    @pl.loop(1, devices)
    def _(o):
        spread_recv(o).wait_recv()

    count = seqs * rows_of // 2
    pairs[:, :rank] = skf[pl.ds(0, count, stride=2), :][:, :rank]
    pairs[:, rank:] = skf[pl.ds(1, count, stride=2), :][:, :rank]
    tiles = rows_of // 2

    def add(t, sums):
        tile = qs[:, pl.ds(pl.multiple_of(t * 2 * rank, 128), 2 * rank)].astype(F32)
        return tuple(
            sums[s] + tile * pairs[pl.ds(s * tiles + t, 1), :] for s in range(seqs)
        )

    zero = jnp.zeros((qs.shape[0], 2 * rank), F32)
    sums = lax.fori_loop(0, tiles, add, (zero,) * seqs)
    ones = jnp.ones((8, 2 * rank), F32)
    for s in range(seqs):
        scores[s : s + 1, :] = matmul_nt(ones, sums[s], HIGH)[0:1, :]

    @pl.loop(1, devices)
    def _(o):
        spread(o).wait_send()


def fused_fits(hidden_in, w_down, proj_model, devices):
    n = devices // 2
    tokens, narrow = hidden_in.shape
    rank = proj_model.shape[1]
    rows_of = tokens // SEQ * 3 * rank
    return (
        devices % 4 == 0
        and n >= 4
        and (2 * narrow) % 128 == 0
        and rank == 64
        and tokens % (SEQ * 2) == 0
        and (2 * narrow) % (16 * CHUNKS) == 0
        and narrow % 16 == 0
        and w_down.shape[0] % 32 == 0
        and rows_of % (8 * devices) == 0
    )


def on_device_fused(
    hidden_in, w_gate, w_up, w_down, norm_gain, out_cotangent, proj_model, proj_hidden, queries
):
    devices = lax.axis_size("dp")
    n = devices // 2
    half = n // 2
    tokens, narrow = hidden_in.shape
    wide, th = 2 * narrow, tokens // 2
    width, units = w_gate.shape
    rank = proj_model.shape[1]
    seqs = tokens // SEQ
    sk_rows = seqs * 3 * rank
    vmem = pltpu.VMEM
    dma = pltpu.SemaphoreType.DMA
    block = (wide, th)
    scratch = [
        vmem((units, width), BF), vmem((units, width), BF), vmem((units, width), BF),
        vmem((3 * rank, width), BF), vmem((3 * rank, units), BF), vmem(queries.shape, BF),
        vmem((width, tokens), BF), vmem((width, tokens), BF),
        vmem((units, tokens), F32), vmem((units, tokens), F32), vmem((units, tokens), F32),
        vmem((units, tokens), BF), vmem((2 * rank, tokens), F32), vmem((rank, tokens), F32),
        vmem((rank, tokens), F32),
        vmem((2, narrow, th), BF), vmem(block, F32), vmem(block, F32), vmem((wide, 128), F32),
        vmem((2, wide, tokens), F32), vmem((n,) + block, BF), vmem((2, half) + block, BF),
        vmem(block, F32), vmem((n, 8, th), F32),
        vmem((narrow, th), BF), vmem((narrow, th), BF),
        vmem((sk_rows, 128), F32), vmem((devices, sk_rows // devices, 128), F32),
        vmem((sk_rows, 128), F32), vmem((sk_rows // 2, 2 * rank), F32),
        dma((2, n)), dma((6,)), dma((2,)), dma((2,)),
    ]
    scratch += [dma((2, half + 1, CHUNKS))] * 8
    scratch += [dma((n,))] * 2 + [dma((2, half, CHUNKS))] * 2 + [dma((n,))] * 2
    scratch += [dma((devices,))] * 4
    near = pl.BlockSpec(memory_space=pltpu.VMEM)
    far = pl.BlockSpec(memory_space=pl.ANY)
    block_out, scores = pl.pallas_call(
        functools.partial(fused, n),
        out_shape=(
            jax.ShapeDtypeStruct((narrow, tokens), BF),
            jax.ShapeDtypeStruct((seqs, queries.shape[0]), F32),
        ),
        in_specs=[near, near, near] + [far] * 6,
        out_specs=(near, near),
        scratch_shapes=scratch,
        compiler_params=pltpu.CompilerParams(
            collective_id=0, has_side_effects=True, vmem_limit_bytes=VMEM_LIMIT
        ),
    )(
        hidden_in.T, out_cotangent.T, norm_gain[None, :], w_gate.T, w_up.T, w_down,
        proj_model.reshape(3 * rank, width), proj_hidden.reshape(3 * rank, units), queries,
    )
    return block_out.T, scores


VMEM_LIMIT = 63 * 1024 * 1024


def on_device(hidden_in, w_gate, w_up, w_down, norm_gain, out_cotangent, proj_model, *rest):
    form = on_device_plain
    if fused_fits(hidden_in, w_down, proj_model, lax.axis_size("dp")):
        form = on_device_fused
    return form(
        hidden_in, w_gate, w_up, w_down, norm_gain, out_cotangent, proj_model, *rest
    )


def solution(mesh):
    in_specs = (
        P("group", "dp"),
        P(None, "dp"),
        P(None, "dp"),
        P("dp", None),
        P(),
        P("group", "dp"),
        P(),
        P(None, None, "dp"),
        P("dp", None),
    )
    out_specs = (P("group", "dp"), P("group", "dp"))
    return jax.shard_map(
        on_device, mesh=mesh, in_specs=in_specs, out_specs=out_specs, check_vma=False
    )
```

```python
import functools

import jax
import jax.numpy as jnp
from jax import lax
from jax.experimental import pallas as pl
from jax.experimental.pallas import tpu as pltpu
from jax.sharding import PartitionSpec as P

SEQ = 256


epsilon = 1e-06


def contract_last(left_mat, right_mat):
    return lax.dot_general(
        left_mat, right_mat, (((1,), (1,)), ((), ())), preferred_element_type=jnp.float32
    )


def contract_lead(left_mat, right_mat):
    return lax.dot_general(
        left_mat, right_mat, (((0,), (1,)), ((), ())), preferred_element_type=jnp.float32
    )


def pair_sketch(inputs_side, grads_side, seq_count):
    inputs_seq = inputs_side.reshape(seq_count, SEQ, inputs_side.shape[1])
    grads_seq = grads_side.reshape(seq_count, SEQ, grads_side.shape[1])
    return jnp.einsum("stk,stj->skj", inputs_seq, grads_seq, precision=lax.Precision.HIGHEST)


def on_device_plain(
    hidden_in, w_gate, w_up, w_down, norm_gain, out_cotangent, proj_model, proj_hidden, queries
):
    width_cols = hidden_in.shape[1]
    rank = proj_model.shape[1]
    devices = lax.axis_size("dp")
    width = width_cols * devices
    total_rows = hidden_in.shape[0]
    seq_count = total_rows // SEQ
    in_sides = proj_model[0:2].reshape(2 * rank, width)
    out_side = proj_model[2]
    first_col = lax.axis_index("dp") * width_cols
    piece = lax.all_gather(hidden_in, "dp", axis=1, tiled=True)
    gate_value = jnp.dot(piece, w_gate, preferred_element_type=jnp.float32)
    up_value = jnp.dot(piece, w_up, preferred_element_type=jnp.float32)
    projected = contract_last(piece, in_sides)
    in_gate = projected[:, :rank]
    in_up = projected[:, rank:]
    sigmoid_gate = jax.nn.sigmoid(gate_value)
    activated = gate_value * sigmoid_gate
    hidden = (activated * up_value).astype(jnp.bfloat16)
    down_cols = lax.psum_scatter(
        contract_lead(w_down, hidden), "dp", scatter_dimension=0, tiled=True
    )
    gain_cols = lax.dynamic_slice_in_dim(norm_gain, first_col, width_cols, 0)[:, None]
    scaled = gain_cols * jnp.transpose(out_cotangent).astype(jnp.float32)
    square_sums, mixed_sums = lax.psum(
        (jnp.sum(down_cols * down_cols, axis=0), jnp.sum(scaled * down_cols, axis=0)), "dp"
    )
    inv_rms = lax.rsqrt(square_sums / width + epsilon)[None, :]
    mixed_mean = (mixed_sums / width)[None, :]
    block_out = (
        hidden_in.astype(jnp.float32) + jnp.transpose(down_cols * inv_rms * gain_cols)
    ).astype(jnp.bfloat16)
    grad_cols = (inv_rms * (scaled - down_cols * inv_rms * inv_rms * mixed_mean)).astype(
        jnp.bfloat16
    )
    block_cols = lax.all_gather(grad_cols, "dp", axis=0, tiled=True)
    grad_hidden = contract_lead(block_cols, w_down)
    out_down = contract_lead(block_cols, out_side)
    grad_up = (grad_hidden * activated).astype(jnp.bfloat16)
    grad_gate = (
        grad_hidden * up_value * sigmoid_gate * (1.0 + gate_value * (1.0 - sigmoid_gate))
    ).astype(jnp.bfloat16)
    out_gate = contract_last(grad_gate, proj_hidden[0])
    out_up = contract_last(grad_up, proj_hidden[1])
    in_down = contract_last(hidden, proj_hidden[2])
    out_gate, out_up, in_down = lax.psum((out_gate, out_up, in_down), "dp")
    sketch = jnp.stack(
        [
            pair_sketch(in_gate, out_gate, seq_count),
            pair_sketch(in_up, out_up, seq_count),
            pair_sketch(in_down, out_down, seq_count),
        ],
        axis=1,
    )
    flat = sketch.reshape(seq_count, 3 * rank * rank)
    scores = jnp.dot(flat, queries.astype(jnp.float32).T, precision=lax.Precision.HIGHEST)
    return (block_out, scores)


CHUNKS = 2
BF = jnp.bfloat16
F32 = jnp.float32
HIGH = lax.Precision.HIGHEST


def matmul(a, b, precision=None):
    return lax.dot_general(
        a, b, (((1,), (0,)), ((), ())), precision=precision, preferred_element_type=F32
    )


def matmul_nt(a, b, precision=None):
    return lax.dot_general(
        a, b, (((1,), (1,)), ((), ())), precision=precision, preferred_element_type=F32
    )


def matmul_tn(a, b):
    return lax.dot_general(a, b, (((0,), (0,)), ((), ())), preferred_element_type=F32)


def fused(
    n,
    x_in, cot_in, gain, w_gate, w_up, w_down, proj_model, proj_hidden, queries,
    out, scores,
    wg, wu, wd, pm, ph, qs,
    xa, ga, gate, up, gh, hid, ip_t, od_t, id_t,
    xch, xf, cf, gcol, ownf, prt, rsr, down, stats, osend, orecv, skp, rsk, skf, pairs,
    w_sem, m_sem, x_ssem, x_rsem, a_s, a_r, p_s, p_r, b_s, b_r, q_s, q_r,
    d_s, d_r, r_s, r_r, st_s, st_r, k_s, k_r, f_s, f_r,
):
    half = n // 2
    devices = 2 * n
    me = lax.axis_index("dp")
    chip, core = me // 2, lax.rem(me, 2)
    narrow, tokens = x_in.shape
    wide = 2 * narrow
    th = tokens // 2
    fc = wide // CHUNKS
    width = wide * n
    seqs = tokens // SEQ
    rank = od_t.shape[0]
    rows_of = 3 * rank

    def chip_at(pos):
        pos = lax.rem(pos + 2 * n, n)
        return jnp.where(pos < half, 2 * pos, 2 * (n - 1 - pos) + 1)

    even = lax.rem(chip, 2) == 0
    here = jnp.where(even, chip // 2, n - 1 - chip // 2)
    right = chip_at(here + 1) * 2 + core
    left = chip_at(here - 1) * 2 + core
    partner = chip * 2 + 1 - core
    onward = (right, left)

    def cols(q):
        return pl.ds(pl.multiple_of(q * wide, 128), wide)

    def feats(q, ch):
        return pl.ds(pl.multiple_of(q * wide + ch * fc, 16), fc)

    def all_feats(q):
        return pl.ds(pl.multiple_of(q * wide, 16), wide)

    def lanes(whose):
        return pl.ds(pl.multiple_of(whose * th, 128), th)

    def remote(src, dst, ssem, rsem, target):
        return pltpu.make_async_remote_copy(
            src_ref=src, dst_ref=dst, send_sem=ssem, recv_sem=rsem,
            device_id={"dp": target}, device_id_type=pl.DeviceIdType.MESH,
        )

    def weight_copy(which, q):
        src, dst = ((w_gate, wg), (w_up, wu))[which]
        return pltpu.make_async_copy(src.at[:, cols(q)], dst.at[:, cols(q)], w_sem.at[which, q])

    def block_chip(i):
        hop = (i + 1) // 2
        return jnp.where(lax.rem(i, 2) == 1, chip_at(here - hop), chip_at(here + hop))

    pm_copy = pltpu.make_async_copy(proj_model, pm, m_sem.at[0])
    ph_copy = pltpu.make_async_copy(proj_hidden, ph, m_sem.at[1])
    wd_copy = pltpu.make_async_copy(w_down, wd, m_sem.at[2])
    q_copy = pltpu.make_async_copy(queries, qs, m_sem.at[3])
    for which in range(2):
        weight_copy(which, chip).start()
    pm_copy.start()

    @pl.loop(1, n)
    def _(i):
        for which in range(2):
            weight_copy(which, block_chip(i)).start()

    wd_copy.start()
    ph_copy.start()
    q_copy.start()

    barrier = pltpu.get_barrier_semaphore()

    @pl.loop(1, devices)
    def _(o):
        pl.semaphore_signal(
            barrier, inc=1, device_id={"dp": lax.rem(me + o, devices)},
            device_id_type=pl.DeviceIdType.MESH,
        )

    pl.semaphore_wait(barrier, devices - 1)

    trades = []
    for at, ref in enumerate((x_in, cot_in)):
        trades.append(
            remote(ref.at[:, lanes(1 - core)], xch.at[at], x_ssem.at[at], x_rsem.at[at], partner)
        )
        trades[-1].start()
    for ref in (gate, up, gh, ip_t, od_t, skp):
        ref[...] = jnp.zeros_like(ref)

    def join(at, ref, dst):
        trades[at].wait_recv()
        dst[own_feats, :] = ref[:, lanes(core)].astype(F32)
        dst[other_feats, :] = xch[at].astype(F32)

    own_feats = pl.ds(pl.multiple_of(core * narrow, 16), narrow)
    other_feats = pl.ds(pl.multiple_of((1 - core) * narrow, 16), narrow)
    join(0, x_in, xf)
    xa[all_feats(chip), lanes(core)] = xf[...].astype(BF)

    def gather(buf, ssem, rsem, psend, precv, compute, before_loop):
        def hop(direction, at, ch, q):
            ref = buf.at[feats(q, ch), lanes(core)]
            where = (direction, at, ch)
            return remote(ref, ref, ssem.at[where], rsem.at[where], onward[direction])

        def last_hop(direction, ch, q):
            ref = buf.at[feats(q, ch), lanes(core)]
            return remote(
                ref, ref, ssem.at[0, half, ch], rsem.at[0, half, ch], onward[direction]
            )

        def share(direction, at, ch, q, whose):
            ref = buf.at[feats(q, ch), lanes(whose)]
            where = (direction, at, ch)
            return remote(ref, ref, psend.at[where], precv.at[where], partner)

        for ch in range(CHUNKS):
            for direction in range(2):
                hop(direction, 1, ch, chip).start()
        for ch in range(CHUNKS):
            share(0, 0, ch, chip, core).start()
        before_loop()
        for ch in range(CHUNKS):
            share(0, 0, ch, chip, 1 - core).wait_recv()
        def pass_on(at, ch):
            for direction in range(2):
                q = chip_at(here - at) if direction == 0 else chip_at(here + at)
                hop(direction, at, ch, q).wait_recv()

                @pl.when(at < half - 1)
                def _():
                    hop(direction, at + 1, ch, q).start()

                @pl.when((at == half - 1) & (core == direction))
                def _():
                    last_hop(direction, ch, q).start()

                share(direction, at, ch, q, core).start()

        compute(chip)
        pass_on(1, 0)

        @pl.loop(1, n)
        def _(i):
            at = (i + 1) // 2
            odd = lax.rem(i, 2) == 1

            @pl.when(odd & (at < half))
            def _():
                for ch in range(1, CHUNKS):
                    pass_on(at, ch)

            @pl.when(jnp.logical_not(odd) & (at + 1 < half))
            def _():
                pass_on(at + 1, 0)

            @pl.when(i == n - 1)
            def _():
                q = chip_at(here - half)
                for ch in range(CHUNKS):
                    last_hop(0, ch, q).wait_recv()
                    share(0, half, ch, q, core).start()

            q = block_chip(i)
            for ch in range(CHUNKS):
                share(1 - lax.rem(i, 2), at, ch, q, 1 - core).wait_recv()
            compute(q)

        def drain():
            for ch in range(CHUNKS):
                share(0, 0, ch, chip, core).wait_send()
                for direction in range(2):
                    for at in range(1, half):
                        back = at - 1 if direction == 0 else 1 - at
                        hop(direction, at, ch, chip_at(here - back)).wait_send()
                        share(direction, at, ch, chip, core).wait_send()
                last_hop(0, ch, chip).wait_send()
                share(0, half, ch, chip, core).wait_send()

        return drain

    def forward(q):
        for which in range(2):
            weight_copy(which, q).wait()
        block = xa[all_feats(q), :]
        gate[...] += matmul(wg[:, cols(q)], block)
        up[...] += matmul(wu[:, cols(q)], block)
        ip_t[...] += matmul(pm[: 2 * rank, cols(q)], block)

    def first_prep():
        join(1, cot_in, cf)
        gcol[...] = jnp.transpose(jnp.broadcast_to(gain[:, cols(chip)], (128, wide)))
        cf[...] = gcol[:, 0:1] * cf[...]
        pm_copy.wait()

    drain = gather(xa, a_s, a_r, p_s, p_r, forward, first_prep)

    piece = 32

    @pl.loop(0, gate.shape[0] // piece)
    def _(i):
        span = pl.ds(pl.multiple_of(i * piece, 16), piece)
        g = gate[span, :]
        u = up[span, :]
        s = jax.nn.sigmoid(g)
        act = g * s
        hid[span, :] = (act * u).astype(BF)
        gate[span, :] = act
        up[span, :] = u * s * (1.0 + g * (1.0 - s))

    drain()
    wd_copy.wait()

    def dest(j):
        far = half - (j + 1) // 2
        away = jnp.where(lax.rem(j, 2) == 1, far, -far)
        return jnp.where(
            j == 0, chip_at(here + half), jnp.where(j == n - 1, chip, chip_at(here + away))
        )

    def part_copy(j, q):
        return remote(
            xa.at[all_feats(q), lanes(1 - core)], prt.at[j], d_s.at[j], d_r.at[j], partner
        )

    def part(j):
        q = dest(j)
        slot = lax.rem(j, 2)
        ownf[slot] = matmul_tn(wd[:, cols(q)], hid[...])
        xa[all_feats(q), lanes(1 - core)] = ownf[slot, :, lanes(1 - core)].astype(BF)
        part_copy(j, q).start()

    def ring_sum(direction, step, ch, q):
        return remote(
            xa.at[feats(q, ch), lanes(core)],
            rsr.at[direction, step, pl.ds(ch * fc, fc), :],
            r_s.at[direction, step, ch],
            r_r.at[direction, step, ch],
            onward[direction],
        )

    def own_sum(j, ch):
        span = pl.ds(ch * fc, fc)
        return ownf[lax.rem(j, 2), span, lanes(core)] + prt[j, span, :].astype(F32)

    def finish(j):
        q = dest(j)
        part_copy(j, q).wait_recv()

        @pl.when(j == 0)
        def _():
            for ch in range(CHUNKS):
                xa[feats(q, ch), lanes(core)] = own_sum(j, ch).astype(BF)
                for direction in range(2):

                    @pl.when(core == direction)
                    def _():
                        ring_sum(direction, 0, ch, q).start()

        step = (j + 1) // 2
        for direction in range(2):

            @pl.when((j > 0) & (lax.rem(j, 2) == 1 - direction))
            def _():
                for ch in range(CHUNKS):
                    span = pl.ds(ch * fc, fc)
                    carried = (step > 1) | (core == direction)

                    @pl.when(carried)
                    def _():
                        ring_sum(direction, step - 1, ch, q).wait_recv()
                        xa[feats(q, ch), lanes(core)] = (
                            own_sum(j, ch) + rsr[direction, step - 1, span, :].astype(F32)
                        ).astype(BF)

                    @pl.when(jnp.logical_not(carried))
                    def _():
                        xa[feats(q, ch), lanes(core)] = own_sum(j, ch).astype(BF)

                    ring_sum(direction, step, ch, q).start()

    part(0)

    @pl.loop(1, n)
    def _(j):
        part(j)
        finish(j - 1)

    part_copy(n - 1, chip).wait_recv()
    for ch in range(CHUNKS):
        span = pl.ds(ch * fc, fc)
        for direction in range(2):
            ring_sum(direction, half - 1, ch, chip).wait_recv()
        down[span, :] = (
            own_sum(n - 1, ch)
            + rsr[0, half - 1, span, :].astype(F32)
            + rsr[1, half - 1, span, :].astype(F32)
        )

    def fold(v):
        return jnp.sum(v, axis=0, keepdims=True)

    stats[chip] = jnp.concatenate(
        [fold(down[...] * down[...]), fold(cf[...] * down[...]), jnp.zeros((6, th), F32)], axis=0
    )

    def stat_copy(o):
        other = lax.rem(chip + o, n)
        ref = stats.at[chip]
        return remote(ref, ref, st_s.at[o], st_r.at[o], other * 2 + core)

    def stat_recv(o):
        ref = stats.at[lax.rem(chip + n - o, n)]
        return remote(ref, ref, st_s.at[o], st_r.at[o], partner)

    for o in range(1, n):
        stat_copy(o).start()
    for o in range(1, n):
        stat_recv(o).wait_recv()
    total = stats[0]
    for at in range(1, n):
        total = total + stats[at]
    inv_rms = lax.rsqrt(total[0:1] / width + epsilon)
    mixed_mean = total[1:2] / width
    normed = down[...] * inv_rms
    ga[all_feats(chip), lanes(core)] = (
        inv_rms * (cf[...] - normed * (inv_rms * mixed_mean))
    ).astype(BF)

    out_copy = remote(osend, orecv, m_sem.at[4], m_sem.at[5], partner)

    def block_output():
        xf[...] = xf[...] + down[...] * inv_rms * gcol[:, 0:1]
        osend[...] = xf[other_feats, :].astype(BF)
        out_copy.start()
        out[:, lanes(core)] = xf[own_feats, :].astype(BF)
        ph_copy.wait()
        id_t[...] = matmul(ph[2 * rank :, :], hid[...])

    def backward(q):
        block = ga[all_feats(q), :]
        gh[...] += matmul(wd[:, cols(q)], block)
        od_t[...] += matmul(pm[2 * rank :, cols(q)], block)

    drain = gather(ga, b_s, b_r, q_s, q_r, backward, block_output)

    out_gate = matmul(ph[:rank, :], (gh[...] * up[...]).astype(BF))
    out_up = matmul(ph[rank : 2 * rank, :], (gh[...] * gate[...]).astype(BF))
    for s in range(seqs):
        at = slice(s * SEQ, (s + 1) * SEQ)
        first = s * rows_of
        skp[first : first + rank, :rank] = matmul_nt(ip_t[:rank, at], out_gate[:, at], HIGH)
        skp[first + rank : first + 2 * rank, :rank] = matmul_nt(
            ip_t[rank:, at], out_up[:, at], HIGH
        )
        skp[first + 2 * rank : first + 3 * rank, :rank] = matmul_nt(
            id_t[:, at], od_t[:, at], HIGH
        )

    share = seqs * rows_of // devices

    def share_rows(d):
        return pl.ds(pl.multiple_of(d * share, 8), share)

    def scatter(o):
        to = lax.rem(me + o, devices)
        return remote(skp.at[share_rows(to), :], rsk.at[o], k_s.at[o], k_r.at[o], to)

    @pl.loop(1, devices)
    def _(o):
        scatter(o).start()

    rsk[0] = skp[share_rows(me), :]

    @pl.loop(1, devices)
    def _(o):
        scatter(o).wait_recv()

    summed = rsk[0]
    for o in range(1, devices):
        summed = summed + rsk[o]
    skf[share_rows(me), :] = summed

    def spread(o):
        ref = skf.at[share_rows(me), :]
        return remote(ref, ref, f_s.at[o], f_r.at[o], lax.rem(me + o, devices))

    def spread_recv(o):
        ref = skf.at[share_rows(lax.rem(me + devices - o, devices)), :]
        return remote(ref, ref, f_s.at[o], f_r.at[o], partner)

    @pl.loop(1, devices)
    def _(o):
        spread(o).start()

    out_copy.wait_recv()
    out[:, lanes(1 - core)] = orecv[...]

    drain()
    out_copy.wait_send()
    for trade in trades:
        trade.wait_send()
    for j in range(n):
        part_copy(j, chip).wait_send()
    for ch in range(CHUNKS):
        for direction in range(2):
            for step in range(1, half):
                ring_sum(direction, step, ch, chip).wait_send()

            @pl.when(core == direction)
            def _():
                ring_sum(direction, 0, ch, chip).wait_send()

    for o in range(1, n):
        stat_copy(o).wait_send()

    @pl.loop(1, devices)
    def _(o):
        scatter(o).wait_send()

    q_copy.wait()

    @pl.loop(1, devices)
    def _(o):
        spread_recv(o).wait_recv()

    count = seqs * rows_of // 2
    pairs[:, :rank] = skf[pl.ds(0, count, stride=2), :][:, :rank]
    pairs[:, rank:] = skf[pl.ds(1, count, stride=2), :][:, :rank]
    tiles = rows_of // 2

    def add(t, sums):
        tile = qs[:, pl.ds(pl.multiple_of(t * 2 * rank, 128), 2 * rank)].astype(F32)
        return tuple(
            sums[s] + tile * pairs[pl.ds(s * tiles + t, 1), :] for s in range(seqs)
        )

    zero = jnp.zeros((qs.shape[0], 2 * rank), F32)
    sums = lax.fori_loop(0, tiles, add, (zero,) * seqs, unroll=8)
    ones = jnp.ones((8, 2 * rank), F32)
    for s in range(seqs):
        scores[s : s + 1, :] = matmul_nt(ones, sums[s], HIGH)[0:1, :]

    @pl.loop(1, devices)
    def _(o):
        spread(o).wait_send()


def fused_fits(hidden_in, w_down, proj_model, devices):
    n = devices // 2
    tokens, narrow = hidden_in.shape
    rank = proj_model.shape[1]
    rows_of = tokens // SEQ * 3 * rank
    return (
        devices % 4 == 0
        and n >= 4
        and (2 * narrow) % 128 == 0
        and rank == 64
        and tokens % (SEQ * 2) == 0
        and (2 * narrow) % (16 * CHUNKS) == 0
        and narrow % 16 == 0
        and w_down.shape[0] % 32 == 0
        and rows_of % (8 * devices) == 0
    )


def on_device_fused(
    hidden_in, w_gate, w_up, w_down, norm_gain, out_cotangent, proj_model, proj_hidden, queries
):
    devices = lax.axis_size("dp")
    n = devices // 2
    half = n // 2
    tokens, narrow = hidden_in.shape
    wide, th = 2 * narrow, tokens // 2
    width, units = w_gate.shape
    rank = proj_model.shape[1]
    seqs = tokens // SEQ
    sk_rows = seqs * 3 * rank
    vmem = pltpu.VMEM
    dma = pltpu.SemaphoreType.DMA
    block = (wide, th)
    scratch = [
        vmem((units, width), BF), vmem((units, width), BF), vmem((units, width), BF),
        vmem((3 * rank, width), BF), vmem((3 * rank, units), BF), vmem(queries.shape, BF),
        vmem((width, tokens), BF), vmem((width, tokens), BF),
        vmem((units, tokens), F32), vmem((units, tokens), F32), vmem((units, tokens), F32),
        vmem((units, tokens), BF), vmem((2 * rank, tokens), F32), vmem((rank, tokens), F32),
        vmem((rank, tokens), F32),
        vmem((2, narrow, th), BF), vmem(block, F32), vmem(block, F32), vmem((wide, 128), F32),
        vmem((2, wide, tokens), F32), vmem((n,) + block, BF), vmem((2, half) + block, BF),
        vmem(block, F32), vmem((n, 8, th), F32),
        vmem((narrow, th), BF), vmem((narrow, th), BF),
        vmem((sk_rows, 128), F32), vmem((devices, sk_rows // devices, 128), F32),
        vmem((sk_rows, 128), F32), vmem((sk_rows // 2, 2 * rank), F32),
        dma((2, n)), dma((6,)), dma((2,)), dma((2,)),
    ]
    scratch += [dma((2, half + 1, CHUNKS))] * 8
    scratch += [dma((n,))] * 2 + [dma((2, half, CHUNKS))] * 2 + [dma((n,))] * 2
    scratch += [dma((devices,))] * 4
    near = pl.BlockSpec(memory_space=pltpu.VMEM)
    far = pl.BlockSpec(memory_space=pl.ANY)
    block_out, scores = pl.pallas_call(
        functools.partial(fused, n),
        out_shape=(
            jax.ShapeDtypeStruct((narrow, tokens), BF),
            jax.ShapeDtypeStruct((seqs, queries.shape[0]), F32),
        ),
        in_specs=[near, near, near] + [far] * 6,
        out_specs=(near, near),
        scratch_shapes=scratch,
        compiler_params=pltpu.CompilerParams(
            collective_id=0, has_side_effects=True, vmem_limit_bytes=VMEM_LIMIT
        ),
    )(
        hidden_in.T, out_cotangent.T, norm_gain[None, :], w_gate.T, w_up.T, w_down,
        proj_model.reshape(3 * rank, width), proj_hidden.reshape(3 * rank, units), queries,
    )
    return block_out.T, scores


VMEM_LIMIT = 63 * 1024 * 1024


def on_device(hidden_in, w_gate, w_up, w_down, norm_gain, out_cotangent, proj_model, *rest):
    form = on_device_plain
    if fused_fits(hidden_in, w_down, proj_model, lax.axis_size("dp")):
        form = on_device_fused
    return form(
        hidden_in, w_gate, w_up, w_down, norm_gain, out_cotangent, proj_model, *rest
    )


def solution(mesh):
    in_specs = (
        P("group", "dp"),
        P(None, "dp"),
        P(None, "dp"),
        P("dp", None),
        P(),
        P("group", "dp"),
        P(),
        P(None, None, "dp"),
        P("dp", None),
    )
    out_specs = (P("group", "dp"), P("group", "dp"))
    return jax.shard_map(
        on_device, mesh=mesh, in_specs=in_specs, out_specs=out_specs, check_vma=False
    )
```
